256 devices in a mesh: row: 16 (over y, x_hi, core), col: 16 (over x_lo, z).
Axes of the slice: x: 4 (x_hi: 2, x_lo: 2; x = x_hi * 2 + x_lo), y: 4, z: 8, core: 2. Of those that a mesh axis runs over, the one named last changes fastest.
Arguments:
- grad_out: bfloat16 [65536, 256], P(('row', 'col')), may hold values from -6 to 6
- pre_act: bfloat16 [65536, 256], P(('row', 'col')), may hold values from -6 to 6
- features: bfloat16 [16, 4096, 256], P('col', 'row'), may hold values from -6 to 6
- weight: bfloat16 [256, 256], replicated, may hold values from -0.375 to 0.375
- tiles: bfloat16 [16, 16, 256, 128, 128], P('row', 'col'), may hold values from -0.078125 to 0.078125
- live: int32 [16, 16], P('row', 'col'), may hold values from 64 to 256, as said below
- block_row: int32 [16, 16, 256], P('row', 'col'), may hold values from 0 to 31, as said below
- block_col: int32 [16, 16, 256], P('row', 'col'), may hold values from 0 to 31
Outputs:
- grad_features: bfloat16 [16, 4096, 256], P('col', 'row')
- grad_weight: float32 [256, 256], replicated
The draws below stay inside these ranges and needn't reach their ends.
Inputs may be any that keep to these rules, and one draw needn't show every extreme that they name: `live`: one tile has exactly 256 nonzero blocks. Within one tile the 256 pairs (block_row, block_col) are all different.
All inputs are finite; a program needn't handle non-finite values.
Results may differ from the reference program's by a relative error of at most 0.02.
Values may be sent and summed in bfloat16 or wider, within the bound.
A program may use at most 128 MiB of HBM per device.

```python
import jax
import jax.numpy as jnp
from jax import lax

F = 256
BLK = 128
NODES = 65536
ROWBLK = 4096
COLBLK = 4096
TBR = 32
TBC = 32
NBLK = 256
N_ROW = 16
N_COL = 16


def shared_slots(key):
    keys = jax.random.split(key, N_ROW * N_COL)

    def one_tile(tile_key):
        return jax.random.permutation(tile_key, TBR * TBC)[:NBLK]
    return jax.vmap(one_tile)(keys).reshape(N_ROW, N_COL, NBLK).astype(jnp.int32)


def draw_block_row(key, part):
    slots = shared_slots(key)
    return slots // TBC


def draw_block_col(key, part):
    slots = shared_slots(key)
    return slots % TBC


def draw_live(key, part):
    key = jax.random.fold_in(key, 3)
    count_key, pick_key = jax.random.split(key)
    counts = jax.random.randint(count_key, (N_ROW * N_COL,), NBLK // 4, NBLK + 1)
    chosen = jax.random.randint(pick_key, (), 0, N_ROW * N_COL)
    counts = counts.at[chosen].set(NBLK)
    return counts.reshape(N_ROW, N_COL).astype(jnp.int32)


def block_levels(own_key, dims, shards, least, top_value):
    level = 1.0
    for position, shards_of in shards:
        steps = jax.random.uniform(jax.random.fold_in(jax.random.fold_in(own_key, 6), position), (shards_of,), jnp.float32, least / len(shards), top_value / len(shards))
        level = level * jnp.repeat(jnp.exp(steps), dims[position] // shards_of).reshape((-1,) + (1,) * (len(dims) - 1 - position))
    return level


def normal_values(own_key, shape, spread, most, cuts=(), kind=jnp.bfloat16):
    gain = block_levels(own_key, shape, cuts, -0.22, 0.18) if cuts else 1.0
    values = jax.random.normal(own_key, shape, jnp.float32) * spread * gain
    return jnp.minimum(jnp.maximum(values, -most), most).astype(kind)


def setup_inputs(seed: int = 0) -> dict:
    splits = jax.random.split(jax.random.key(seed), 9)
    grad_out = normal_values(splits[0], (NODES, F), 1.0, 6.0, ((0, 256),))
    pre_act = normal_values(splits[1], (NODES, F), 1.0, 6.0, ((0, 256),))
    features = normal_values(splits[2], (N_COL, COLBLK, F), 1.0, 6.0, ((0, 16), (1, 16)))
    weight = normal_values(splits[3], (F, F), F ** -0.5, 0.375)
    tiles = normal_values(splits[4], (N_ROW, N_COL, NBLK, BLK, BLK), (NBLK * BLK * N_ROW // (3 * TBC)) ** -0.5, 0.078125, ((0, 16), (1, 16)))
    live = draw_live(jax.random.fold_in(splits[8], 71), 0)
    block_row = draw_block_row(jax.random.fold_in(splits[8], 71), 0)
    block_col = draw_block_col(jax.random.fold_in(splits[8], 71), 0)
    return dict(grad_out=grad_out, pre_act=pre_act, features=features, weight=weight, tiles=tiles, live=live, block_row=block_row, block_col=block_col)


def tile_term(grad_block, tile_set, rows_idx, cols_idx, count):
    row_blocks = grad_block.reshape(TBR, BLK, F)
    gathered = row_blocks[rows_idx]
    contrib = jnp.einsum("guv,guf->gvf", tile_set.astype(jnp.float32), gathered.astype(jnp.float32), precision=lax.Precision.HIGHEST)
    keep = jnp.arange(NBLK, dtype=jnp.int32) < count
    contrib = jnp.where(keep[:, None, None], contrib, 0.0)
    summed = jax.ops.segment_sum(contrib, cols_idx, num_segments=TBC)
    return summed.reshape(COLBLK, F).astype(jnp.bfloat16)


def reference(grad_out, pre_act, features, weight, tiles, live, block_row, block_col):
    grad_pre = jnp.where(pre_act > 0, grad_out, jnp.zeros_like(grad_out))
    grad_blocks = grad_pre.reshape(N_ROW, ROWBLK, F)

    def row_step(total, index):
        def one_tile(other):
            return tile_term(grad_blocks[index], tiles[index, other], block_row[index, other], block_col[index, other], live[index, other]).astype(jnp.float32)

        terms = lax.map(one_tile, jnp.arange(N_COL, dtype=jnp.int32))
        return total + terms, None

    start_total = jnp.zeros((N_COL, COLBLK, F), jnp.float32)
    back, unused = lax.scan(row_step, start_total, jnp.arange(N_ROW, dtype=jnp.int32))
    back_rounded = back.astype(jnp.bfloat16).reshape(NODES, F)
    grad_features = jnp.dot(back_rounded, weight.T, preferred_element_type=jnp.float32).astype(jnp.bfloat16)
    grad_weight = jnp.dot(features.reshape(NODES, F).astype(jnp.float32).T, back.reshape(NODES, F), precision=lax.Precision.HIGHEST)
    grad_weight = grad_weight * (NODES ** -0.5)
    return grad_features.reshape(N_COL, COLBLK, F), grad_weight
```

```python
import functools

import jax
import jax.numpy as jnp
from jax import lax
from jax.experimental import pallas as pl
from jax.experimental.pallas import tpu as pltpu
from jax.sharding import PartitionSpec as P

MESH = pl.DeviceIdType.MESH
F32 = jnp.float32
BF16 = jnp.bfloat16

F = 256
B = 128
NB = 32
LISTED = 256
NR = 16
NC = 16
STEPS = 4

N_AG = 34


def kernel(go_ref, pre_ref, feat_ref, w_ref, tiles_ref, live_ref, brow_ref, bcol_ref,
           gf_ref, gw_ref,
           tiles_v, gt, acc, idx_v, idx_s, featt, wt,
           sb1, rb1, ysend, yrecv, xsend, xrecv,
           gsum, grow, grow_in, gcol, gcol_in, gall,
           tile_sem, idx_sem, ag_send, ag_recv, s1_send, s1_recv, y_send, y_recv, x_send, x_recv,
           r_send, r_recv, c_send, c_recv, b_send, b_recv):
    i = lax.axis_index("row")
    j = lax.axis_index("col")
    y, xh, c = i // 4, (i // 2) % 2, i % 2
    xl, z = j // 8, j % 8

    def row_of(yy, xx, cc):
        return (yy * 2 + xx) * 2 + cc

    z_up = (i, xl * 8 + (z + 1) % 8)
    z_dn = (i, xl * 8 + (z + 7) % 8)
    x_peer = (i, (1 - xl) * 8 + z)
    core_peer = (row_of(y, xh, 1 - c), j)
    y_up = (row_of((y + 1) % 4, xh, c), j)
    y_dn = (row_of((y + 3) % 4, xh, c), j)
    xh_peer = (row_of(y, 1 - xh, c), j)

    tile_copy = pltpu.make_async_copy(tiles_ref.at[0, 0], tiles_v.at[pl.ds(0, LISTED)], tile_sem)
    tile_copy.start()

    barrier = pltpu.get_barrier_semaphore()

    @pl.loop(1, 16)
    def _(d):
        pl.semaphore_signal(barrier, inc=1, device_id=((i + d) % NR, j), device_id_type=MESH)
        pl.semaphore_signal(barrier, inc=1, device_id=(i, (j + d) % NC), device_id_type=MESH)

    g = jnp.where(pre_ref[...] > 0, go_ref[...], jnp.zeros_like(go_ref[...]))
    gT = g.T
    gt[2 * j] = gT[:, :B]
    gt[2 * j + 1] = gT[:, B:]

    pl.semaphore_wait(barrier, 30)

    sends = []

    def blk(dz, cls):
        zz = (z + dz + 16) % 8
        side = xl if cls in "AB" else 1 - xl
        return 2 * (side * 8 + zz) + (1 if cls in "BQ" else 0)

    def send(block, half, target, k):
        if half is None:
            src = gt.at[block]
        else:
            src = gt.at[block, pl.ds(half * B, B)]
        d = pltpu.make_async_remote_copy(src_ref=src, dst_ref=src, send_sem=ag_send.at[k], recv_sem=ag_recv.at[k],
                                         device_id=target, device_id_type=MESH)
        d.start()
        sends.append(d)
        return d

    CLS = "BAP"
    handle = {}

    def push(cls, s, src_up, src_dn):
        ci = CLS.index(cls)
        half_u = 0 if s == STEPS else None
        half_d = 1 if s == STEPS else None
        handle[(cls, s, "u")] = send(blk(src_up, cls), half_u, z_up, ci * 4 + s - 1)
        handle[(cls, s, "d")] = send(blk(src_dn, cls), half_d, z_dn, 12 + ci * 4 + s - 1)

    xa = send(blk(0, "A"), None, x_peer, 24)
    push("B", 1, 0, 0)
    push("A", 1, 0, 0)
    xb = {0: [send(blk(0, "B"), None, x_peer, 25)]}

    key = brow_ref[0] * NB + bcol_ref[0]
    lane = lax.broadcasted_iota(jnp.int32, (1, LISTED), 1)
    key = jnp.where(lane < live_ref[0, 0], key, -1)
    for h in range(2):
        kt = jnp.broadcast_to(key[:, h * B:(h + 1) * B], (B, B)).T
        number = lax.broadcasted_iota(jnp.int32, (B, B), 0) + h * B
        cell = lax.broadcasted_iota(jnp.int32, (B, B), 1)
        for q in range(8):
            found = jnp.where(kt == cell + q * B, number, LISTED)
            best = jnp.min(found, axis=0, keepdims=True)
            if h == 0:
                idx_v[q:q + 1, :] = best
            else:
                idx_v[q:q + 1, :] = jnp.minimum(idx_v[q:q + 1, :], best)
    idx_copy = pltpu.make_async_copy(idx_v, idx_s, idx_sem)
    idx_copy.start()
    tiles_v[LISTED] = jnp.zeros((B, B), BF16)
    featt[...] = feat_ref[0].T
    wt[...] = w_ref[...].T

    def product(blocks, d):
        parts_l, parts_r = [], []
        for b in blocks:
            parts_l.append(gt[b])
            q, o = b // 4, (b % 4) * NB
            left = tiles_v[idx_s[q, o + 2 * d]]
            right = tiles_v[idx_s[q, o + 2 * d + 1]]
            parts_r.append(jnp.concatenate([left, right], axis=1))
        return jnp.dot(jnp.concatenate(parts_l, axis=1), jnp.concatenate(parts_r, axis=0), preferred_element_type=F32)

    def blocks_of(s):
        if s == 0 or s == STEPS:
            return [blk(s, k) for k in "ABPQ"]
        return [blk(t, k) for t in (s, -s) for k in "ABPQ"]

    def work(s, lo, hi):
        blocks = blocks_of(s)

        @pl.loop(lo, hi)
        def _(d):
            v = product(blocks, d)
            if s == 0:
                acc[d] = v
            else:
                acc[d] += v

    cuts = (0, 5, 10, 16)
    idx_copy.wait()
    tile_copy.wait()
    xa.wait_recv()
    push("P", 1, 0, 0)
    for s in range(1, STEPS + 1):
        for n, cls in enumerate(CLS):
            handle[(cls, s, "u")].wait_recv()
            handle[(cls, s, "d")].wait_recv()
            if s < STEPS:
                push(cls, s + 1, -s, s)
            if cls == "B":
                if s < STEPS:
                    xb[s] = [send(blk(-s, "B"), None, x_peer, 24 + 2 * s), send(blk(s, "B"), None, x_peer, 25 + 2 * s)]
                else:
                    xb[s] = [send(blk(s, "B"), 0, x_peer, 24 + 2 * s), send(blk(s, "B"), 1, x_peer, 25 + 2 * s)]
                for d in xb[s - 1]:
                    d.wait_recv()
            work(s - 1, cuts[n], cuts[n + 1])
    for d in xb[STEPS]:
        d.wait_recv()

    last = blocks_of(STEPS)
    DY = (2, 1, 3, 0)

    def core_copy(m):
        return pltpu.make_async_remote_copy(src_ref=sb1.at[m], dst_ref=rb1.at[m], send_sem=s1_send.at[m], recv_sem=s1_recv.at[m],
                                            device_id=core_peer, device_id_type=MESH)

    def dest(m, cc):
        p = m // 2
        dy = (2 + 3 * p + (p // 2) * 3 + (p // 3) * 2) % 4
        return row_of((y + dy) % 4, m % 2, cc)

    @pl.loop(0, 8)
    def _(m):
        d = dest(m, 1 - c)
        sb1[m] = (acc[d] + product(last, d)).astype(BF16)
        core_copy(m).start()

    @pl.loop(0, 8)
    def _(m):
        d = dest(m, c)
        acc[d] += product(last, d)

    def mine(m):
        return acc.at[dest(m, c)]

    ysends = []

    def y_copy(k, target):
        d = pltpu.make_async_remote_copy(src_ref=ysend.at[k], dst_ref=yrecv.at[k], send_sem=y_send.at[k], recv_sem=y_recv.at[k],
                                         device_id=target, device_id_type=MESH)
        d.start()
        ysends.append(d)
        return d

    h_a, h_b = pl.ds(0, B), pl.ds(B, B)
    yh = {}
    for m in range(8):
        core_copy(m).wait_recv()
        a = mine(m)
        p, xx = m // 2, m % 2
        if p == 0:
            v = (a[...] + rb1[m].astype(F32)).astype(BF16)
            ysend[0 + xx] = v[:B]
            yh[0 + xx] = y_copy(0 + xx, y_up)
            ysend[2 + xx] = v[B:]
            yh[2 + xx] = y_copy(2 + xx, y_dn)
        elif p == 1:
            v = a[...] + rb1[m].astype(F32)
            ysend[4 + xx] = v[B:].astype(BF16)
            yh[4 + xx] = y_copy(4 + xx, y_up)
            a[h_a, :] = v[:B]
        elif p == 2:
            v = a[...] + rb1[m].astype(F32)
            ysend[6 + xx] = v[:B].astype(BF16)
            yh[6 + xx] = y_copy(6 + xx, y_dn)
            a[h_b, :] = v[B:]
        else:
            a[...] += rb1[m].astype(F32)
    for xx in range(2):
        yh[0 + xx].wait_recv()
        ysend[8 + xx] = (mine(2 + xx)[h_a, :] + yrecv[0 + xx].astype(F32)).astype(BF16)
        yh[8 + xx] = y_copy(8 + xx, y_up)
        yh[2 + xx].wait_recv()
        ysend[10 + xx] = (mine(4 + xx)[h_b, :] + yrecv[2 + xx].astype(F32)).astype(BF16)
        yh[10 + xx] = y_copy(10 + xx, y_dn)
    for k in (4, 5, 6, 7, 8, 9, 10, 11):
        yh[k].wait_recv()

    def y_sum(xx, keep):
        top = acc[keep, h_a, :] + yrecv[6 + xx].astype(F32) + yrecv[8 + xx].astype(F32)
        bot = acc[keep, h_b, :] + yrecv[4 + xx].astype(F32) + yrecv[10 + xx].astype(F32)
        return top, bot

    def y_total(xx):
        keep = row_of(y, xx, c)
        top = acc[keep, h_a, :] + yrecv[6 + xx].astype(F32) + yrecv[8 + xx].astype(F32)
        bot = acc[keep, h_b, :] + yrecv[4 + xx].astype(F32) + yrecv[10 + xx].astype(F32)
        return top, bot

    top, bot = y_total(1 - xh)
    xsend[0:B] = top.astype(BF16)
    xsend[B:] = bot.astype(BF16)
    xc = pltpu.make_async_remote_copy(src_ref=xsend, dst_ref=xrecv, send_sem=x_send, recv_sem=x_recv,
                                      device_id=xh_peer, device_id_type=MESH)
    xc.start()
    top, bot = y_total(xh)
    xc.wait_recv()
    back = jnp.concatenate([top, bot], axis=0) + xrecv[...].astype(F32)
    back_t = back.astype(BF16).T
    gsum[...] = jnp.dot(featt[...], back_t, preferred_element_type=F32)
    gf_ref[0] = jnp.dot(back_t, wt[...], preferred_element_type=F32).astype(BF16)

    grow[...] = gsum[...].astype(BF16)

    def r_copy(d):
        to = (i + d) % NR
        return pltpu.make_async_remote_copy(src_ref=grow.at[pl.ds(pl.multiple_of(to * 16, 16), 16)], dst_ref=grow_in.at[d],
                                            send_sem=r_send.at[d], recv_sem=r_recv.at[d], device_id=(to, j), device_id_type=MESH)

    @pl.loop(1, NR)
    def _(d):
        r_copy(d).start()

    total = gsum[pl.ds(pl.multiple_of(i * 16, 16), 16), :]
    for d in range(1, NR):
        r_copy(d).wait_recv()
        total += grow_in[d].astype(F32)
    gcol[...] = total.astype(BF16)
    gcol_in[j] = total.astype(BF16)

    def c_copy(d):
        to = (j + d) % NC
        return pltpu.make_async_remote_copy(src_ref=gcol, dst_ref=gcol_in.at[j],
                                            send_sem=c_send.at[d], recv_sem=c_recv.at[d], device_id=(i, to), device_id_type=MESH)

    @pl.loop(1, NC)
    def _(d):
        c_copy(d).start()

    @pl.loop(1, NC)
    def _(d):
        c_copy(d).wait_recv()

    total = gcol_in[0].astype(F32)
    for d in range(1, NC):
        total += gcol_in[d].astype(F32)
    gall[i] = (total * (1.0 / 256.0)).astype(BF16)

    def b_copy(d):
        to = (i + d) % NR
        return pltpu.make_async_remote_copy(src_ref=gall.at[i], dst_ref=gall.at[i],
                                            send_sem=b_send.at[d], recv_sem=b_recv.at[d], device_id=(to, j), device_id_type=MESH)

    @pl.loop(1, NR)
    def _(d):
        b_copy(d).start()

    @pl.loop(1, NR)
    def _(d):
        b_copy(d).wait_recv()

    for d in range(NR):
        gw_ref[d * 16:(d + 1) * 16, :] = gall[d].astype(F32)

    for d in sends:
        d.wait_send()
    for d in ysends:
        d.wait_send()
    xc.wait_send()

    @pl.loop(0, 8)
    def _(m):
        core_copy(m).wait_send()

    @pl.loop(1, NR)
    def _(d):
        r_copy(d).wait_send()
        c_copy(d).wait_send()
        b_copy(d).wait_send()


def shards(grad_out, pre_act, features, weight, tiles, live, block_row, block_col):
    vmem = pl.BlockSpec(memory_space=pltpu.VMEM)
    return pl.pallas_call(
        kernel,
        out_shape=(jax.ShapeDtypeStruct((1, 256, F), BF16), jax.ShapeDtypeStruct((F, F), F32)),
        in_specs=[vmem, vmem, vmem, vmem, pl.BlockSpec(memory_space=pl.ANY), pl.BlockSpec(memory_space=pltpu.SMEM), vmem, vmem],
        out_specs=(vmem, vmem),
        scratch_shapes=[
            pltpu.VMEM((LISTED + 1, B, B), BF16),
            pltpu.VMEM((NB, F, B), BF16),
            pltpu.VMEM((NR, F, F), F32),
            pltpu.VMEM((8, B), jnp.int32),
            pltpu.SMEM((8, B), jnp.int32),
            pltpu.VMEM((F, F), BF16),
            pltpu.VMEM((F, F), BF16),
            pltpu.VMEM((8, F, F), BF16),
            pltpu.VMEM((8, F, F), BF16),
            pltpu.VMEM((12, B, F), BF16),
            pltpu.VMEM((12, B, F), BF16),
            pltpu.VMEM((F, F), BF16),
            pltpu.VMEM((F, F), BF16),
            pltpu.VMEM((F, F), F32),
            pltpu.VMEM((F, F), BF16),
            pltpu.VMEM((NR, 16, F), BF16),
            pltpu.VMEM((16, F), BF16),
            pltpu.VMEM((NC, 16, F), BF16),
            pltpu.VMEM((NR, 16, F), BF16),
            pltpu.SemaphoreType.DMA,
            pltpu.SemaphoreType.DMA,
            pltpu.SemaphoreType.DMA((N_AG,)),
            pltpu.SemaphoreType.DMA((N_AG,)),
            pltpu.SemaphoreType.DMA((8,)),
            pltpu.SemaphoreType.DMA((8,)),
            pltpu.SemaphoreType.DMA((12,)),
            pltpu.SemaphoreType.DMA((12,)),
            pltpu.SemaphoreType.DMA,
            pltpu.SemaphoreType.DMA,
            pltpu.SemaphoreType.DMA((NR,)),
            pltpu.SemaphoreType.DMA((NR,)),
            pltpu.SemaphoreType.DMA((NC,)),
            pltpu.SemaphoreType.DMA((NC,)),
            pltpu.SemaphoreType.DMA((NR,)),
            pltpu.SemaphoreType.DMA((NR,)),
        ],
        compiler_params=pltpu.CompilerParams(collective_id=0, has_side_effects=True, vmem_limit_bytes=48 * 1024 * 1024),
        cost_estimate=pl.CostEstimate(flops=2 * 4096 * 4096 * 256, bytes_accessed=10 * 1024 * 1024, transcendentals=0),
    )(grad_out, pre_act, features, weight, tiles, live, block_row, block_col)


def solution(mesh):
    in_specs = (
        P(("row", "col"), None),
        P(("row", "col"), None),
        P("col", "row", None),
        P(),
        P("row", "col", None, None, None),
        P("row", "col"),
        P("row", "col", None),
        P("row", "col", None),
    )
    out_specs = (P("col", "row", None), P())
    return jax.shard_map(shards, mesh=mesh, in_specs=in_specs, out_specs=out_specs, check_vma=False)
```

```python
import functools

import jax
import jax.numpy as jnp
from jax import lax
from jax.experimental import pallas as pl
from jax.experimental.pallas import tpu as pltpu
from jax.sharding import PartitionSpec as P

MESH = pl.DeviceIdType.MESH
F32 = jnp.float32
BF16 = jnp.bfloat16

F = 256
B = 128
NB = 32
LISTED = 256
NR = 16
NC = 16
STEPS = 4

N_AG = 34


def kernel(go_hbm, pre_hbm, feat_hbm, w_hbm, tiles_ref, live_ref, brow_hbm, bcol_hbm,
           gf_ref, gw_ref,
           go_ref, pre_ref, w_ref, brow_ref, bcol_ref, in_sem,
           tiles_v, gt, acc, idx_v, idx_s, fv, wt,
           pb, rb1, yrecv,
           gsum, grow, grow_in, gcol_in, gall,
           tile_sem, idx_sem, ag_send, ag_recv, f_send, f_recv, s1_send, s1_recv, y_send, y_recv,
           r_send, r_recv, c_send, c_recv, b_send, b_recv):
    i = lax.axis_index("row")
    j = lax.axis_index("col")
    y, xh, c = i // 4, (i // 2) % 2, i % 2
    xl, z = j // 8, j % 8

    def row_of(yy, xx, cc):
        return (yy * 2 + xx) * 2 + cc

    z_up = (i, xl * 8 + (z + 1) % 8)
    z_dn = (i, xl * 8 + (z + 7) % 8)
    x_peer = (i, (1 - xl) * 8 + z)
    core_peer = (row_of(y, xh, 1 - c), j)
    y_up = (row_of((y + 1) % 4, xh, c), j)
    y_dn = (row_of((y + 3) % 4, xh, c), j)
    xh_peer = (row_of(y, 1 - xh, c), j)

    loads = [pltpu.make_async_copy(a, b, in_sem.at[k]) for k, (a, b) in enumerate((
        (go_hbm, go_ref), (pre_hbm, pre_ref), (brow_hbm, brow_ref), (bcol_hbm, bcol_ref), (feat_hbm.at[0], fv.at[i]), (w_hbm, w_ref)))]
    for load in loads:
        load.start()
    tile_copy = pltpu.make_async_copy(tiles_ref.at[0, 0], tiles_v.at[pl.ds(0, LISTED)], tile_sem)
    tile_copy.start()

    barrier = pltpu.get_barrier_semaphore()

    for near_by in (z_up, z_dn, x_peer, core_peer, y_up, y_dn, xh_peer):
        pl.semaphore_signal(barrier, inc=1, device_id=near_by, device_id_type=MESH)

    loads[0].wait()
    loads[1].wait()
    g = jnp.where(pre_ref[...] > 0, go_ref[...], jnp.zeros_like(go_ref[...]))
    gT = g.T
    gt[2 * j] = gT[:, :B]
    gt[2 * j + 1] = gT[:, B:]

    pl.semaphore_wait(barrier, 7)

    sends = []

    def blk(dz, cls):
        zz = (z + dz + 16) % 8
        side = xl if cls in "AB" else 1 - xl
        return 2 * (side * 8 + zz) + (1 if cls in "BQ" else 0)

    def send(block, half, target, k):
        if half is None:
            src = gt.at[block]
        else:
            src = gt.at[block, pl.ds(half * B, B)]
        d = pltpu.make_async_remote_copy(src_ref=src, dst_ref=src, send_sem=ag_send.at[k], recv_sem=ag_recv.at[k],
                                         device_id=target, device_id_type=MESH)
        d.start()
        sends.append(d)
        return d

    CLS = "BAP"
    handle = {}

    def push(cls, s, src_up, src_dn):
        ci = CLS.index(cls)
        half_u = 0 if s == STEPS else None
        half_d = 1 if s == STEPS else None
        handle[(cls, s, "u")] = send(blk(src_up, cls), half_u, z_up, ci * 4 + s - 1)
        handle[(cls, s, "d")] = send(blk(src_dn, cls), half_d, z_dn, 12 + ci * 4 + s - 1)

    xa = send(blk(0, "A"), None, x_peer, 24)
    push("B", 1, 0, 0)
    push("A", 1, 0, 0)
    xb = {0: [send(blk(0, "B"), None, x_peer, 25)]}

    for load in (loads[2], loads[3], loads[5]):
        load.wait()
    key = brow_ref[0] * NB + bcol_ref[0]
    lane = lax.broadcasted_iota(jnp.int32, (1, LISTED), 1)
    key = jnp.where(lane < live_ref[0, 0], key, -1)
    for h in range(2):
        kt = jnp.broadcast_to(key[:, h * B:(h + 1) * B], (B, B)).T
        number = lax.broadcasted_iota(jnp.int32, (B, B), 0) + h * B
        cell = lax.broadcasted_iota(jnp.int32, (B, B), 1)
        for q in range(8):
            found = jnp.where(kt == cell + q * B, number, LISTED)
            best = jnp.min(found, axis=0, keepdims=True)
            if h == 0:
                idx_v[q:q + 1, :] = best
            else:
                idx_v[q:q + 1, :] = jnp.minimum(idx_v[q:q + 1, :], best)
    idx_copy = pltpu.make_async_copy(idx_v, idx_s, idx_sem)
    idx_copy.start()
    tiles_v[LISTED] = jnp.zeros((B, B), BF16)
    wt[...] = w_ref[...].T

    def product(blocks, d):
        parts_l, parts_r = [], []
        for b in blocks:
            parts_l.append(gt[b])
            q, o = b // 4, (b % 4) * NB
            left = tiles_v[idx_s[q, o + 2 * d]]
            right = tiles_v[idx_s[q, o + 2 * d + 1]]
            parts_r.append(jnp.concatenate([left, right], axis=1))
        return jnp.dot(jnp.concatenate(parts_l, axis=1), jnp.concatenate(parts_r, axis=0), preferred_element_type=F32)

    def blocks_of(s):
        if s == 0 or s == STEPS:
            return [blk(s, k) for k in "ABPQ"]
        return [blk(t, k) for t in (s, -s) for k in "ABPQ"]

    def work(s, lo, hi, classes=None):
        blocks = blocks_of(s) if classes is None else [blk(s, k) for k in classes]

        @pl.loop(lo, hi, unroll=hi - lo)
        def _(d):
            v = product(blocks, d)
            if s == 0:
                acc[d] = v
            else:
                acc[d] += v

    fsends = []

    def fcopy(row, half, target, k):
        src = fv.at[row] if half is None else fv.at[row, pl.ds(half * B, B)]
        d = pltpu.make_async_remote_copy(src_ref=src, dst_ref=src, send_sem=f_send.at[k], recv_sem=f_recv.at[k],
                                         device_id=target, device_id_type=MESH)
        d.start()
        fsends.append(d)
        return d

    def near(dy, q):
        return row_of((y + dy + 4) % 4, (xh + q) % 2, c)

    def fpush(q, k):
        return fcopy(near(0, q), None, y_up, k), fcopy(near(0, q), None, y_dn, k + 1)

    def fcore(dy, q, k):
        return fcopy(near(dy, q), None, core_peer, k)

    loads[4].wait()
    f_x = fcopy(i, None, xh_peer, 0)
    f_own = fpush(0, 1)
    to_core = [fcore(0, 0, 9)]
    f_far = []

    def feature_step(n, f_x_):
        if n == 0:
            f_x_.wait_recv()
            pushed.append(fpush(1, 3))
            to_core.append(fcore(0, 1, 10))
        elif n == 1:
            for q in range(2):
                up, dn = (f_own, pushed[0])[q]
                up.wait_recv()
                f_far.append(fcopy(near(-1, q), 0, y_up, 5 + 2 * q))
                dn.wait_recv()
                f_far.append(fcopy(near(1, q), 1, y_dn, 6 + 2 * q))
                to_core.append(fcore(-1, q, 11 + 2 * q))
                to_core.append(fcore(1, q, 12 + 2 * q))
        else:
            for d in f_far:
                d.wait_recv()
            for q in range(2):
                to_core.append(fcore(2, q, 15 + q))

    pushed = []

    cuts = (0, 5, 10, 16)
    idx_copy.wait()
    tile_copy.wait()
    xa.wait_recv()
    push("P", 1, 0, 0)
    for s in range(1, STEPS + 1):
        for n, cls in enumerate(CLS):
            handle[(cls, s, "u")].wait_recv()
            handle[(cls, s, "d")].wait_recv()
            if s < STEPS:
                push(cls, s + 1, -s, s)
            if cls == "B":
                if s < STEPS:
                    xb[s] = [send(blk(-s, "B"), None, x_peer, 24 + 2 * s), send(blk(s, "B"), None, x_peer, 25 + 2 * s)]
                else:
                    xb[s] = [send(blk(s, "B"), 0, x_peer, 24 + 2 * s), send(blk(s, "B"), 1, x_peer, 25 + 2 * s)]
                for d in xb[s - 1]:
                    d.wait_recv()
            if cls == "A" and s > 1:
                feature_step(s - 2, f_x)
            work(s - 1, cuts[n], cuts[n + 1])
    for d in xb[STEPS]:
        d.wait_recv()

    last = blocks_of(STEPS)
    ORDER = ((2, 1), (2, 0), (1, 1), (3, 1), (0, 1), (1, 0), (3, 0), (0, 0))

    def core_copy(m):
        return pltpu.make_async_remote_copy(src_ref=pb.at[dest(m, 1 - c)], dst_ref=rb1.at[m], send_sem=s1_send.at[m], recv_sem=s1_recv.at[m],
                                            device_id=core_peer, device_id_type=MESH)

    def dest(m, cc):
        dy, q = ORDER[m]
        return row_of((y + dy) % 4, (xh + q) % 2, cc)

    for m in range(8):
        d = dest(m, 1 - c)
        pb[d] = (acc[d] + product(last, d)).astype(BF16)
        core_copy(m).start()
    for m in range(8):
        d = dest(m, c)
        pb[d] = (acc[d] + product(last, d)).astype(BF16)

    def each(copies, what):
        for copy in copies:
            getattr(copy, what)()

    for d in to_core:
        d.wait_recv()
    gt_sum = None
    for k in range(4):
        left = jnp.concatenate([pb[4 * k + n] for n in range(4)], axis=1)
        right = jnp.concatenate([fv[4 * k + n] for n in range(4)], axis=0)
        v = jnp.dot(left, right, preferred_element_type=F32)
        gt_sum = v if gt_sum is None else gt_sum + v
    gsum[...] = gt_sum.T
    grow[...] = gsum[...].astype(BF16)

    one, two = i, j

    def at(p, q):
        return (p, q)

    def r_copy(d):
        to = (one + d) % NR
        return pltpu.make_async_remote_copy(src_ref=grow.at[pl.ds(pl.multiple_of(to * 16, 16), 16)], dst_ref=grow_in.at[d],
                                            send_sem=r_send.at[d], recv_sem=r_recv.at[d], device_id=at(to, two), device_id_type=MESH)

    r_copies = [r_copy(d) for d in range(1, NR)]
    each(r_copies, "start")

    def y_copy(m):
        dy, q = ORDER[m]
        return pltpu.make_async_remote_copy(src_ref=pb.at[dest(m, c)], dst_ref=yrecv.at[m], send_sem=y_send.at[m], recv_sem=y_recv.at[m],
                                            device_id=(dest(m, c), j), device_id_type=MESH)

    core_copies = [core_copy(m) for m in range(8)]
    y_copies = [y_copy(m) for m in range(7)]
    for m in range(8):
        core_copies[m].wait_recv()
        d = dest(m, c)
        if m < 7:
            pb[d] = (pb[d].astype(F32) + rb1[m].astype(F32)).astype(BF16)
            y_copies[m].start()
        else:
            acc[d] = pb[d].astype(F32) + rb1[m].astype(F32)

    total = gsum[pl.ds(pl.multiple_of(one * 16, 16), 16), :]
    for n, copy in enumerate(r_copies):
        copy.wait_recv()
        total += grow_in[n + 1].astype(F32)
    gcol_in[two] = total.astype(BF16)

    def c_copy(d):
        to = (two + d) % NC
        return pltpu.make_async_remote_copy(src_ref=gcol_in.at[two], dst_ref=gcol_in.at[two],
                                            send_sem=c_send.at[d], recv_sem=c_recv.at[d], device_id=at(one, to), device_id_type=MESH)

    c_copies = [c_copy(d) for d in range(1, NC)]
    each(c_copies, "start")
    each(c_copies, "wait_recv")
    total = gcol_in[0].astype(F32)
    for d in range(1, NC):
        total += gcol_in[d].astype(F32)
    gall[one] = (total * (1.0 / 256.0)).astype(BF16)

    def b_copy(d):
        to = (one + d) % NR
        return pltpu.make_async_remote_copy(src_ref=gall.at[one], dst_ref=gall.at[one],
                                            send_sem=b_send.at[d], recv_sem=b_recv.at[d], device_id=at(to, two), device_id_type=MESH)

    b_copies = [b_copy(d) for d in range(1, NR)]
    each(b_copies, "start")

    each(y_copies, "wait_recv")
    back = acc[i]
    for m in range(7):
        back += yrecv[m].astype(F32)
    gf_ref[0] = jnp.dot(back.astype(BF16).T, wt[...], preferred_element_type=F32).astype(BF16)

    each(b_copies, "wait_recv")
    for d in range(NR):
        gw_ref[d * 16:(d + 1) * 16, :] = gall[d].astype(F32)

    each(sends + fsends + core_copies + y_copies + r_copies + c_copies + b_copies, "wait_send")


def shards(grad_out, pre_act, features, weight, tiles, live, block_row, block_col):
    vmem = pl.BlockSpec(memory_space=pltpu.VMEM)
    hbm = pl.BlockSpec(memory_space=pltpu.HBM)
    return pl.pallas_call(
        kernel,
        out_shape=(pltpu.VMEM((1, 256, F), BF16), pltpu.VMEM((F, F), F32)),
        in_specs=[hbm, hbm, hbm, hbm, hbm, pl.BlockSpec(memory_space=pltpu.SMEM), hbm, hbm],
        out_specs=(vmem, vmem),
        scratch_shapes=[
            pltpu.VMEM((256, F), BF16),
            pltpu.VMEM((256, F), BF16),
            pltpu.VMEM((F, F), BF16),
            pltpu.VMEM((1, 1, LISTED), jnp.int32),
            pltpu.VMEM((1, 1, LISTED), jnp.int32),
            pltpu.SemaphoreType.DMA((6,)),
            pltpu.VMEM((LISTED + 1, B, B), BF16),
            pltpu.VMEM((NB, F, B), BF16),
            pltpu.VMEM((NR, F, F), F32),
            pltpu.VMEM((8, B), jnp.int32),
            pltpu.SMEM((8, B), jnp.int32),
            pltpu.VMEM((NR, 256, F), BF16),
            pltpu.VMEM((F, F), BF16),
            pltpu.VMEM((NR, F, F), BF16),
            pltpu.VMEM((8, F, F), BF16),
            pltpu.VMEM((7, F, F), BF16),
            pltpu.VMEM((F, F), F32),
            pltpu.VMEM((F, F), BF16),
            pltpu.VMEM((NR, 16, F), BF16),
            pltpu.VMEM((NC, 16, F), BF16),
            pltpu.VMEM((NR, 16, F), BF16),
            pltpu.SemaphoreType.DMA,
            pltpu.SemaphoreType.DMA,
            pltpu.SemaphoreType.DMA((N_AG,)),
            pltpu.SemaphoreType.DMA((N_AG,)),
            pltpu.SemaphoreType.DMA((17,)),
            pltpu.SemaphoreType.DMA((17,)),
            pltpu.SemaphoreType.DMA((8,)),
            pltpu.SemaphoreType.DMA((8,)),
            pltpu.SemaphoreType.DMA((7,)),
            pltpu.SemaphoreType.DMA((7,)),
            pltpu.SemaphoreType.DMA((NR,)),
            pltpu.SemaphoreType.DMA((NR,)),
            pltpu.SemaphoreType.DMA((NC,)),
            pltpu.SemaphoreType.DMA((NC,)),
            pltpu.SemaphoreType.DMA((NR,)),
            pltpu.SemaphoreType.DMA((NR,)),
        ],
        compiler_params=pltpu.CompilerParams(collective_id=0, has_side_effects=True, vmem_limit_bytes=56 * 1024 * 1024),
        cost_estimate=pl.CostEstimate(flops=2 * 4096 * 4096 * 256, bytes_accessed=10 * 1024 * 1024, transcendentals=0),
    )(grad_out, pre_act, features, weight, tiles, live, block_row, block_col)


def solution(mesh):
    in_specs = (
        P(("row", "col"), None),
        P(("row", "col"), None),
        P("col", "row", None),
        P(),
        P("row", "col", None, None, None),
        P("row", "col"),
        P("row", "col", None),
        P("row", "col", None),
    )
    out_specs = (P("col", "row", None), P())
    return jax.shard_map(shards, mesh=mesh, in_specs=in_specs, out_specs=out_specs, check_vma=False)
```

```python
import functools

import jax
import jax.numpy as jnp
from jax import lax
from jax.experimental import pallas as pl
from jax.experimental.pallas import tpu as pltpu
from jax.sharding import PartitionSpec as P

MESH = pl.DeviceIdType.MESH
F32 = jnp.float32
BF16 = jnp.bfloat16

F = 256
B = 128
NB = 32
LISTED = 256
NR = 16
NC = 16
STEPS = 4

N_AG = 34


def kernel(go_hbm, pre_hbm, feat_hbm, w_hbm, tiles_ref, live_ref, brow_hbm, bcol_hbm,
           gf_ref, gw_ref,
           go_ref, pre_ref, w_ref, brow_ref, bcol_ref, in_sem,
           tiles_v, gt, acc, idx_v, idx_s, fv, wt,
           pb, rb1, yrecv,
           gsum, grow, grow_in, gcol_in, gall,
           tile_sem, idx_sem, ag_send, ag_recv, f_send, f_recv, s1_send, s1_recv, y_send, y_recv,
           r_send, r_recv, c_send, c_recv, b_send, b_recv):
    i = lax.axis_index("row")
    j = lax.axis_index("col")
    y, xh, c = i // 4, (i // 2) % 2, i % 2
    xl, z = j // 8, j % 8

    def row_of(yy, xx, cc):
        return (yy * 2 + xx) * 2 + cc

    z_up = (i, xl * 8 + (z + 1) % 8)
    z_dn = (i, xl * 8 + (z + 7) % 8)
    x_peer = (i, (1 - xl) * 8 + z)
    core_peer = (row_of(y, xh, 1 - c), j)
    y_up = (row_of((y + 1) % 4, xh, c), j)
    y_dn = (row_of((y + 3) % 4, xh, c), j)
    xh_peer = (row_of(y, 1 - xh, c), j)

    loads = [pltpu.make_async_copy(a, b, in_sem.at[k]) for k, (a, b) in enumerate((
        (go_hbm, go_ref), (pre_hbm, pre_ref), (brow_hbm, brow_ref), (bcol_hbm, bcol_ref), (feat_hbm.at[0], fv.at[i]), (w_hbm, w_ref)))]
    for load in loads:
        load.start()
    tile_copy = pltpu.make_async_copy(tiles_ref.at[0, 0], tiles_v.at[pl.ds(0, LISTED)], tile_sem)
    tile_copy.start()

    barrier = pltpu.get_barrier_semaphore()

    for near_by in (z_up, z_dn, x_peer, core_peer, y_up, y_dn, xh_peer):
        pl.semaphore_signal(barrier, inc=1, device_id=near_by, device_id_type=MESH)

    loads[0].wait()
    loads[1].wait()
    g = jnp.where(pre_ref[...] > 0, go_ref[...], jnp.zeros_like(go_ref[...]))
    gT = g.T
    gt[2 * j] = gT[:, :B]
    gt[2 * j + 1] = gT[:, B:]

    pl.semaphore_wait(barrier, 7)

    sends = []

    def blk(dz, cls):
        zz = (z + dz + 16) % 8
        side = xl if cls in "AB" else 1 - xl
        return 2 * (side * 8 + zz) + (1 if cls in "BQ" else 0)

    def send(block, half, target, k):
        if half is None:
            src = gt.at[block]
        else:
            src = gt.at[block, pl.ds(half * B, B)]
        d = pltpu.make_async_remote_copy(src_ref=src, dst_ref=src, send_sem=ag_send.at[k], recv_sem=ag_recv.at[k],
                                         device_id=target, device_id_type=MESH)
        d.start()
        sends.append(d)
        return d

    CLS = "BAP"
    handle = {}

    def push(cls, s, src_up, src_dn):
        ci = CLS.index(cls)
        half_u = 0 if s == STEPS else None
        half_d = 1 if s == STEPS else None
        handle[(cls, s, "u")] = send(blk(src_up, cls), half_u, z_up, ci * 4 + s - 1)
        handle[(cls, s, "d")] = send(blk(src_dn, cls), half_d, z_dn, 12 + ci * 4 + s - 1)

    xa = send(blk(0, "A"), None, x_peer, 24)
    push("B", 1, 0, 0)
    push("A", 1, 0, 0)
    xb = {0: [send(blk(0, "B"), None, x_peer, 25)]}

    for load in (loads[2], loads[3], loads[5]):
        load.wait()
    key = brow_ref[0] * NB + bcol_ref[0]
    lane = lax.broadcasted_iota(jnp.int32, (1, LISTED), 1)
    key = jnp.where(lane < live_ref[0, 0], key, -1)
    for h in range(2):
        kt = jnp.broadcast_to(key[:, h * B:(h + 1) * B], (B, B)).T
        number = lax.broadcasted_iota(jnp.int32, (B, B), 0) + h * B
        cell = lax.broadcasted_iota(jnp.int32, (B, B), 1)
        for q in range(8):
            found = jnp.where(kt == cell + q * B, number, LISTED)
            best = jnp.min(found, axis=0, keepdims=True)
            if h == 0:
                idx_v[q:q + 1, :] = best
            else:
                idx_v[q:q + 1, :] = jnp.minimum(idx_v[q:q + 1, :], best)
    idx_copy = pltpu.make_async_copy(idx_v, idx_s, idx_sem)
    idx_copy.start()
    tiles_v[LISTED] = jnp.zeros((B, B), BF16)
    wt[...] = w_ref[...].T

    def product(blocks, d):
        parts_l, parts_r = [], []
        for b in blocks:
            parts_l.append(gt[b])
            q, o = b // 4, (b % 4) * NB
            left = tiles_v[idx_s[q, o + 2 * d]]
            right = tiles_v[idx_s[q, o + 2 * d + 1]]
            parts_r.append(jnp.concatenate([left, right], axis=1))
        return jnp.dot(jnp.concatenate(parts_l, axis=1), jnp.concatenate(parts_r, axis=0), preferred_element_type=F32)

    def blocks_of(s):
        if s == 0 or s == STEPS:
            return [blk(s, k) for k in "ABPQ"]
        return [blk(t, k) for t in (s, -s) for k in "ABPQ"]

    def work(s, lo, hi, classes="ABPQ"):
        blocks = [blk(t, k) for t in ((s, -s) if s else (0,)) for k in classes]

        @pl.loop(lo, hi, unroll=hi - lo)
        def _(d):
            v = product(blocks, d)
            if s == 0:
                acc[d] = v
            else:
                acc[d] += v

    fsends = []

    def fcopy(row, half, target, k):
        src = fv.at[row] if half is None else fv.at[row, pl.ds(half * B, B)]
        d = pltpu.make_async_remote_copy(src_ref=src, dst_ref=src, send_sem=f_send.at[k], recv_sem=f_recv.at[k],
                                         device_id=target, device_id_type=MESH)
        d.start()
        fsends.append(d)
        return d

    def near(dy, q):
        return row_of((y + dy + 4) % 4, (xh + q) % 2, c)

    def fpush(q, k):
        return fcopy(near(0, q), None, y_up, k), fcopy(near(0, q), None, y_dn, k + 1)

    def fcore(dy, q, k):
        return fcopy(near(dy, q), None, core_peer, k)

    loads[4].wait()
    f_x = fcopy(i, None, xh_peer, 0)
    f_own = fpush(0, 1)
    to_core = [fcore(0, 0, 9)]
    f_far = {}
    f_xh = []

    def f_around(q):
        up, dn = (f_own, f_xh)[q]
        up.wait_recv()
        far_up = fcopy(near(-1, q), 0, y_up, 5 + 2 * q)
        dn.wait_recv()
        f_far[q] = (far_up, fcopy(near(1, q), 1, y_dn, 6 + 2 * q))
        to_core.append(fcore(-1, q, 11 + 2 * q))
        to_core.append(fcore(1, q, 12 + 2 * q))

    def f_end(q):
        for d in f_far[q]:
            d.wait_recv()
        to_core.append(fcore(2, q, 15 + q))

    def feature_step(s, cls):
        if (s, cls) == (1, "P"):
            f_around(0)
        elif (s, cls) == (2, "B"):
            f_x.wait_recv()
            f_xh.extend(fpush(1, 3))
            to_core.append(fcore(0, 1, 10))
        elif (s, cls) == (3, "A"):
            f_around(1)
            f_end(0)
        elif (s, cls) == (4, "P"):
            f_end(1)

    idx_copy.wait()
    tile_copy.wait()
    xa.wait_recv()
    push("P", 1, 0, 0)
    for s in range(1, STEPS + 1):
        for n, cls in enumerate(CLS):
            handle[(cls, s, "u")].wait_recv()
            handle[(cls, s, "d")].wait_recv()
            if s < STEPS:
                push(cls, s + 1, -s, s)
            if cls == "B":
                if s < STEPS:
                    xb[s] = [send(blk(-s, "B"), None, x_peer, 24 + 2 * s), send(blk(s, "B"), None, x_peer, 25 + 2 * s)]
                else:
                    xb[s] = [send(blk(s, "B"), 0, x_peer, 24 + 2 * s), send(blk(s, "B"), 1, x_peer, 25 + 2 * s)]
                for d in xb[s - 1]:
                    d.wait_recv()
            feature_step(s, cls)
            if n < 2:
                work(s - 1, 8 * n, 8 * n + 8, "PQ" if s > 1 else "ABPQ")
            elif s < STEPS:
                work(s, 0, NR, "AB")
    for d in xb[STEPS]:
        d.wait_recv()

    last = blocks_of(STEPS)
    ORDER = ((2, 1), (2, 0), (1, 1), (3, 1), (0, 1), (1, 0), (3, 0), (0, 0))

    def core_copy(m):
        return pltpu.make_async_remote_copy(src_ref=pb.at[dest(m, 1 - c)], dst_ref=rb1.at[m], send_sem=s1_send.at[m], recv_sem=s1_recv.at[m],
                                            device_id=core_peer, device_id_type=MESH)

    def dest(m, cc):
        dy, q = ORDER[m]
        return row_of((y + dy) % 4, (xh + q) % 2, cc)

    for m in range(8):
        d = dest(m, 1 - c)
        pb[d] = (acc[d] + product(last, d)).astype(BF16)
        core_copy(m).start()
    for m in range(8):
        d = dest(m, c)
        pb[d] = (acc[d] + product(last, d)).astype(BF16)

    def each(copies, what):
        for copy in copies:
            getattr(copy, what)()

    late = to_core.pop()
    spots = [near(dy, q) for dy, q in ((0, 0), (0, 1), (1, 0), (3, 0), (1, 1), (3, 1), (2, 0), (2, 1))]
    spots = [p + o for p in spots for o in (0, 1 - 2 * c)]
    for d in to_core:
        d.wait_recv()
    gt_sum = None
    for k in range(4):
        if k == 3:
            late.wait_recv()
        left = jnp.concatenate([pb[p] for p in spots[4 * k:4 * k + 4]], axis=1)
        right = jnp.concatenate([fv[p] for p in spots[4 * k:4 * k + 4]], axis=0)
        v = jnp.dot(left, right, preferred_element_type=F32)
        gt_sum = v if gt_sum is None else gt_sum + v
    gsum[...] = gt_sum.T
    grow[...] = gsum[...].astype(BF16)

    ROWS = [(dy, q, k) for dy, q in ((2, 1), (1, 1), (3, 1), (2, 0), (0, 1), (1, 0), (3, 0), (0, 0)) for k in (1, 0)][:15]
    COLS = [(dz, k) for dz in (4, 3, 5, 2, 6, 1, 7, 0) for k in (1, 0)][:15]

    def along_row(d):
        dy, q, k = ROWS[d]
        return row_of((y + dy) % 4, (xh + q) % 2, (c + k) % 2)

    def along_col(d):
        dz, k = COLS[d]
        return ((xl + k) % 2) * 8 + (z + dz) % 8

    def r_copy(d):
        to = along_row(d)
        return pltpu.make_async_remote_copy(src_ref=grow.at[pl.ds(pl.multiple_of(to * 16, 16), 16)], dst_ref=grow_in.at[d],
                                            send_sem=r_send.at[d], recv_sem=r_recv.at[d], device_id=(to, j), device_id_type=MESH)

    r_copies = [r_copy(d) for d in range(15)]
    each(r_copies, "start")

    def y_copy(m):
        dy, q = ORDER[m]
        return pltpu.make_async_remote_copy(src_ref=pb.at[dest(m, c)], dst_ref=yrecv.at[m], send_sem=y_send.at[m], recv_sem=y_recv.at[m],
                                            device_id=(dest(m, c), j), device_id_type=MESH)

    core_copies = [core_copy(m) for m in range(8)]
    y_copies = [y_copy(m) for m in range(7)]

    def sums(lo, hi):
        for m in range(lo, hi):
            core_copies[m].wait_recv()
            d = dest(m, c)
            if m < 7:
                pb[d] = (pb[d].astype(F32) + rb1[m].astype(F32)).astype(BF16)
                y_copies[m].start()
            else:
                acc[d] = pb[d].astype(F32) + rb1[m].astype(F32)

    sums(0, 4)

    total = gsum[pl.ds(pl.multiple_of(i * 16, 16), 16), :]
    for n, copy in enumerate(r_copies):
        copy.wait_recv()
        total += grow_in[n].astype(F32)
    gcol_in[j] = total.astype(BF16)

    def c_copy(d):
        to = along_col(d)
        return pltpu.make_async_remote_copy(src_ref=gcol_in.at[j], dst_ref=gcol_in.at[j],
                                            send_sem=c_send.at[d], recv_sem=c_recv.at[d], device_id=(i, to), device_id_type=MESH)

    c_copies = [c_copy(d) for d in range(15)]
    each(c_copies, "start")
    sums(4, 8)
    each(c_copies, "wait_recv")
    total = gcol_in[0].astype(F32)
    for d in range(1, NC):
        total += gcol_in[d].astype(F32)
    gall[i] = (total * (1.0 / 256.0)).astype(BF16)

    def b_copy(d):
        to = along_row(d)
        return pltpu.make_async_remote_copy(src_ref=gall.at[i], dst_ref=gall.at[i],
                                            send_sem=b_send.at[d], recv_sem=b_recv.at[d], device_id=(to, j), device_id_type=MESH)

    b_copies = [b_copy(d) for d in range(15)]
    each(b_copies, "start")

    each(y_copies, "wait_recv")
    back = acc[i]
    for m in range(7):
        back += yrecv[m].astype(F32)
    gf_ref[0] = jnp.dot(back.astype(BF16).T, wt[...], preferred_element_type=F32).astype(BF16)

    each(b_copies, "wait_recv")
    for d in range(NR):
        gw_ref[d * 16:(d + 1) * 16, :] = gall[d].astype(F32)

    each(sends + fsends + core_copies + y_copies + r_copies + c_copies + b_copies, "wait_send")


def shards(grad_out, pre_act, features, weight, tiles, live, block_row, block_col):
    vmem = pl.BlockSpec(memory_space=pltpu.VMEM)
    hbm = pl.BlockSpec(memory_space=pltpu.HBM)
    return pl.pallas_call(
        kernel,
        out_shape=(pltpu.VMEM((1, 256, F), BF16), pltpu.VMEM((F, F), F32)),
        in_specs=[hbm, hbm, hbm, hbm, hbm, pl.BlockSpec(memory_space=pltpu.SMEM), hbm, hbm],
        out_specs=(vmem, vmem),
        scratch_shapes=[
            pltpu.VMEM((256, F), BF16),
            pltpu.VMEM((256, F), BF16),
            pltpu.VMEM((F, F), BF16),
            pltpu.VMEM((1, 1, LISTED), jnp.int32),
            pltpu.VMEM((1, 1, LISTED), jnp.int32),
            pltpu.SemaphoreType.DMA((6,)),
            pltpu.VMEM((LISTED + 1, B, B), BF16),
            pltpu.VMEM((NB, F, B), BF16),
            pltpu.VMEM((NR, F, F), F32),
            pltpu.VMEM((8, B), jnp.int32),
            pltpu.SMEM((8, B), jnp.int32),
            pltpu.VMEM((NR, 256, F), BF16),
            pltpu.VMEM((F, F), BF16),
            pltpu.VMEM((NR, F, F), BF16),
            pltpu.VMEM((8, F, F), BF16),
            pltpu.VMEM((7, F, F), BF16),
            pltpu.VMEM((F, F), F32),
            pltpu.VMEM((F, F), BF16),
            pltpu.VMEM((NR, 16, F), BF16),
            pltpu.VMEM((NC, 16, F), BF16),
            pltpu.VMEM((NR, 16, F), BF16),
            pltpu.SemaphoreType.DMA,
            pltpu.SemaphoreType.DMA,
            pltpu.SemaphoreType.DMA((N_AG,)),
            pltpu.SemaphoreType.DMA((N_AG,)),
            pltpu.SemaphoreType.DMA((17,)),
            pltpu.SemaphoreType.DMA((17,)),
            pltpu.SemaphoreType.DMA((8,)),
            pltpu.SemaphoreType.DMA((8,)),
            pltpu.SemaphoreType.DMA((7,)),
            pltpu.SemaphoreType.DMA((7,)),
            pltpu.SemaphoreType.DMA((NR,)),
            pltpu.SemaphoreType.DMA((NR,)),
            pltpu.SemaphoreType.DMA((NC,)),
            pltpu.SemaphoreType.DMA((NC,)),
            pltpu.SemaphoreType.DMA((NR,)),
            pltpu.SemaphoreType.DMA((NR,)),
        ],
        compiler_params=pltpu.CompilerParams(collective_id=0, has_side_effects=True, vmem_limit_bytes=56 * 1024 * 1024),
        cost_estimate=pl.CostEstimate(flops=2 * 4096 * 4096 * 256, bytes_accessed=10 * 1024 * 1024, transcendentals=0),
    )(grad_out, pre_act, features, weight, tiles, live, block_row, block_col)


def solution(mesh):
    in_specs = (
        P(("row", "col"), None),
        P(("row", "col"), None),
        P("col", "row", None),
        P(),
        P("row", "col", None, None, None),
        P("row", "col"),
        P("row", "col", None),
        P("row", "col", None),
    )
    out_specs = (P("col", "row", None), P())
    return jax.shard_map(shards, mesh=mesh, in_specs=in_specs, out_specs=out_specs, check_vma=False)
```

```python
import functools

import jax
import jax.numpy as jnp
from jax import lax
from jax.experimental import pallas as pl
from jax.experimental.pallas import tpu as pltpu
from jax.sharding import PartitionSpec as P

MESH = pl.DeviceIdType.MESH
F32 = jnp.float32
BF16 = jnp.bfloat16

F = 256
B = 128
NB = 32
LISTED = 256
NR = 16
NC = 16
STEPS = 4

N_AG = 34


def kernel(go_hbm, pre_hbm, feat_hbm, w_hbm, tiles_ref, live_ref, brow_hbm, bcol_hbm,
           gf_ref, gw_ref,
           go_ref, pre_ref, w_ref, brow_ref, bcol_ref, in_sem,
           tiles_v, gt, acc, idx_v, idx_s, fv, wt,
           pb, rb1, yrecv,
           gsum, grow, grow_in, gcol_in, gall,
           tile_sem, idx_sem, ag_send, ag_recv, f_send, f_recv, s1_send, s1_recv, y_send, y_recv,
           r_send, r_recv, c_send, c_recv, b_send, b_recv):
    i = lax.axis_index("row")
    j = lax.axis_index("col")
    y, xh, c = i // 4, (i // 2) % 2, i % 2
    xl, z = j // 8, j % 8

    def row_of(yy, xx, cc):
        return (yy * 2 + xx) * 2 + cc

    z_up = (i, xl * 8 + (z + 1) % 8)
    z_dn = (i, xl * 8 + (z + 7) % 8)
    x_peer = (i, (1 - xl) * 8 + z)
    core_peer = (row_of(y, xh, 1 - c), j)
    y_up = (row_of((y + 1) % 4, xh, c), j)
    y_dn = (row_of((y + 3) % 4, xh, c), j)
    xh_peer = (row_of(y, 1 - xh, c), j)

    loads = [pltpu.make_async_copy(a, b, in_sem.at[k]) for k, (a, b) in enumerate((
        (go_hbm, go_ref), (pre_hbm, pre_ref), (brow_hbm, brow_ref), (bcol_hbm, bcol_ref), (feat_hbm.at[0], fv.at[i]), (w_hbm, w_ref)))]
    for load in loads:
        load.start()
    tile_copy = pltpu.make_async_copy(tiles_ref.at[0, 0], tiles_v.at[pl.ds(0, LISTED)], tile_sem)
    tile_copy.start()

    barrier = pltpu.get_barrier_semaphore()

    for near_by in (z_up, z_dn, x_peer, core_peer, y_up, y_dn, xh_peer):
        pl.semaphore_signal(barrier, inc=1, device_id=near_by, device_id_type=MESH)

    loads[0].wait()
    loads[1].wait()
    g = jnp.where(pre_ref[...] > 0, go_ref[...], jnp.zeros_like(go_ref[...]))
    gT = g.T
    gt[2 * j] = gT[:, :B]
    gt[2 * j + 1] = gT[:, B:]

    pl.semaphore_wait(barrier, 7)

    sends = []

    def blk(dz, cls):
        zz = (z + dz + 16) % 8
        side = xl if cls in "AB" else 1 - xl
        return 2 * (side * 8 + zz) + (1 if cls in "BQ" else 0)

    def send(block, half, target, k):
        if half is None:
            src = gt.at[block]
        else:
            src = gt.at[block, pl.ds(half * B, B)]
        d = pltpu.make_async_remote_copy(src_ref=src, dst_ref=src, send_sem=ag_send.at[k], recv_sem=ag_recv.at[k],
                                         device_id=target, device_id_type=MESH)
        d.start()
        sends.append(d)
        return d

    CLS = "BAP"
    handle = {}

    def push(cls, s, src_up, src_dn):
        ci = CLS.index(cls)
        half_u = 0 if s == STEPS else None
        half_d = 1 if s == STEPS else None
        handle[(cls, s, "u")] = send(blk(src_up, cls), half_u, z_up, ci * 4 + s - 1)
        handle[(cls, s, "d")] = send(blk(src_dn, cls), half_d, z_dn, 12 + ci * 4 + s - 1)

    xa = send(blk(0, "A"), None, x_peer, 24)
    push("B", 1, 0, 0)
    push("A", 1, 0, 0)
    xb = {0: [send(blk(0, "B"), None, x_peer, 25)]}

    for load in (loads[2], loads[3], loads[5]):
        load.wait()
    key = brow_ref[0] * NB + bcol_ref[0]
    lane = lax.broadcasted_iota(jnp.int32, (1, LISTED), 1)
    key = jnp.where(lane < live_ref[0, 0], key, -1)
    for h in range(2):
        kt = jnp.broadcast_to(key[:, h * B:(h + 1) * B], (B, B)).T
        number = lax.broadcasted_iota(jnp.int32, (B, B), 0) + h * B
        cell = lax.broadcasted_iota(jnp.int32, (B, B), 1)
        for q in range(8):
            found = jnp.where(kt == cell + q * B, number, LISTED)
            best = jnp.min(found, axis=0, keepdims=True)
            if h == 0:
                idx_v[q:q + 1, :] = best
            else:
                idx_v[q:q + 1, :] = jnp.minimum(idx_v[q:q + 1, :], best)
    idx_copy = pltpu.make_async_copy(idx_v, idx_s, idx_sem)
    idx_copy.start()
    tiles_v[LISTED] = jnp.zeros((B, B), BF16)
    wt[...] = w_ref[...].T

    def product(blocks, d):
        parts_l, parts_r = [], []
        for b in blocks:
            parts_l.append(gt[b])
            q, o = b // 4, (b % 4) * NB
            left = tiles_v[idx_s[q, o + 2 * d]]
            right = tiles_v[idx_s[q, o + 2 * d + 1]]
            parts_r.append(jnp.concatenate([left, right], axis=1))
        return jnp.dot(jnp.concatenate(parts_l, axis=1), jnp.concatenate(parts_r, axis=0), preferred_element_type=F32)

    def blocks_of(s):
        if s == 0 or s == STEPS:
            return [blk(s, k) for k in "ABPQ"]
        return [blk(t, k) for t in (s, -s) for k in "ABPQ"]

    def work(s, lo, hi, classes="ABPQ"):
        blocks = [blk(t, k) for t in ((s, -s) if s else (0,)) for k in classes]

        @pl.loop(lo, hi, unroll=hi - lo)
        def _(d):
            v = product(blocks, d)
            if s == 0:
                acc[d] = v
            else:
                acc[d] += v

    fsends = []

    def fcopy(row, half, target, k):
        src = fv.at[row] if half is None else fv.at[row, pl.ds(half * B, B)]
        d = pltpu.make_async_remote_copy(src_ref=src, dst_ref=src, send_sem=f_send.at[k], recv_sem=f_recv.at[k],
                                         device_id=target, device_id_type=MESH)
        d.start()
        fsends.append(d)
        return d

    def near(dy, q):
        return row_of((y + dy + 4) % 4, (xh + q) % 2, c)

    def fpush(q, k):
        return fcopy(near(0, q), None, y_up, k), fcopy(near(0, q), None, y_dn, k + 1)

    def fcore(dy, q, k):
        return fcopy(near(dy, q), None, core_peer, k)

    loads[4].wait()
    f_x = fcopy(i, None, xh_peer, 0)
    f_own = fpush(0, 1)
    to_core = [fcore(0, 0, 9)]
    f_far = {}
    f_xh = []

    def f_around(q):
        up, dn = (f_own, f_xh)[q]
        up.wait_recv()
        far_up = fcopy(near(-1, q), 0, y_up, 5 + 2 * q)
        dn.wait_recv()
        f_far[q] = (far_up, fcopy(near(1, q), 1, y_dn, 6 + 2 * q))
        to_core.append(fcore(-1, q, 11 + 2 * q))
        to_core.append(fcore(1, q, 12 + 2 * q))

    def f_end(q):
        for d in f_far[q]:
            d.wait_recv()
        to_core.append(fcore(2, q, 15 + q))

    def feature_step(s, cls):
        if (s, cls) == (1, "P"):
            f_around(0)
        elif (s, cls) == (2, "B"):
            f_x.wait_recv()
            f_xh.extend(fpush(1, 3))
            to_core.append(fcore(0, 1, 10))
        elif (s, cls) == (3, "A"):
            f_around(1)
            f_end(0)
        elif (s, cls) == (4, "P"):
            f_end(1)

    idx_copy.wait()
    tile_copy.wait()
    xa.wait_recv()
    push("P", 1, 0, 0)
    for s in range(1, STEPS + 1):
        for n, cls in enumerate(CLS):
            handle[(cls, s, "u")].wait_recv()
            handle[(cls, s, "d")].wait_recv()
            if s < STEPS:
                push(cls, s + 1, -s, s)
            if cls == "B":
                if s < STEPS:
                    xb[s] = [send(blk(-s, "B"), None, x_peer, 24 + 2 * s), send(blk(s, "B"), None, x_peer, 25 + 2 * s)]
                else:
                    xb[s] = [send(blk(s, "B"), 0, x_peer, 24 + 2 * s), send(blk(s, "B"), 1, x_peer, 25 + 2 * s)]
                for d in xb[s - 1]:
                    d.wait_recv()
            feature_step(s, cls)
            if n < 2:
                work(s - 1, 8 * n, 8 * n + 8, "PQ" if s > 1 else "ABPQ")
            elif s < STEPS:
                work(s, 0, NR, "AB")
    for d in xb[STEPS]:
        d.wait_recv()

    last = blocks_of(STEPS)
    ORDER = ((2, 1), (2, 0), (1, 1), (3, 1), (0, 1), (1, 0), (3, 0), (0, 0))

    def core_copy(m):
        return pltpu.make_async_remote_copy(src_ref=pb.at[dest(m, 1 - c)], dst_ref=rb1.at[m], send_sem=s1_send.at[m], recv_sem=s1_recv.at[m],
                                            device_id=core_peer, device_id_type=MESH)

    def dest(m, cc):
        dy, q = ORDER[m]
        return row_of((y + dy) % 4, (xh + q) % 2, cc)

    for m in range(8):
        d = dest(m, 1 - c)
        pb[d] = (acc[d] + product(last, d)).astype(BF16)
        core_copy(m).start()
    for m in range(8):
        d = dest(m, c)
        pb[d] = (acc[d] + product(last, d)).astype(BF16)

    def each(copies, what):
        for copy in copies:
            getattr(copy, what)()

    late = to_core.pop()
    spots = [near(dy, q) for dy, q in ((0, 0), (0, 1), (1, 0), (3, 0), (1, 1), (3, 1), (2, 0), (2, 1))]
    spots = [p + o for p in spots for o in (0, 1 - 2 * c)]
    for d in to_core:
        d.wait_recv()
    gt_sum = None
    for k in range(4):
        if k == 3:
            late.wait_recv()
        left = jnp.concatenate([pb[p] for p in spots[4 * k:4 * k + 4]], axis=1)
        right = jnp.concatenate([fv[p] for p in spots[4 * k:4 * k + 4]], axis=0)
        v = jnp.dot(left, right, preferred_element_type=F32)
        gt_sum = v if gt_sum is None else gt_sum + v
    gsum[...] = gt_sum.T
    grow[...] = gsum[...].astype(BF16)

    ONES = [(dy, p, k) for dy, p in ((2, 1), (1, 1), (3, 1), (2, 0), (0, 1), (1, 0), (3, 0), (0, 0)) for k in (1, 0)][:15]
    TWOS = [(4, 1), (3, 1), (5, 1), (4, 0), (2, 1), (6, 1), (1, 1), (7, 1), (3, 0), (5, 0), (0, 1), (2, 0), (6, 0), (1, 0), (7, 0)]
    one, two = (y * 2 + xl) * 2 + c, xh * 8 + z

    def along_one(d):
        dy, p, k = ONES[d]
        yy, pp, cc = (y + dy) % 4, (xl + p) % 2, (c + k) % 2
        return (yy * 2 + pp) * 2 + cc, (row_of(yy, xh, cc), pp * 8 + z)

    def along_two(d):
        dz, q = TWOS[d]
        return row_of(y, (xh + q) % 2, c), xl * 8 + (z + dz) % 8

    def r_copy(d):
        to, where = along_one(d)
        return pltpu.make_async_remote_copy(src_ref=grow.at[pl.ds(pl.multiple_of(to * 16, 16), 16)], dst_ref=grow_in.at[d],
                                            send_sem=r_send.at[d], recv_sem=r_recv.at[d], device_id=where, device_id_type=MESH)

    r_copies = [r_copy(d) for d in range(15)]
    each(r_copies, "start")

    def y_copy(m):
        dy, q = ORDER[m]
        return pltpu.make_async_remote_copy(src_ref=pb.at[dest(m, c)], dst_ref=yrecv.at[m], send_sem=y_send.at[m], recv_sem=y_recv.at[m],
                                            device_id=(dest(m, c), j), device_id_type=MESH)

    core_copies = [core_copy(m) for m in range(8)]
    y_copies = [y_copy(m) for m in range(7)]

    def sums(lo, hi):
        for m in range(lo, hi):
            core_copies[m].wait_recv()
            d = dest(m, c)
            if m < 7:
                pb[d] = (pb[d].astype(F32) + rb1[m].astype(F32)).astype(BF16)
                y_copies[m].start()
            else:
                acc[d] = pb[d].astype(F32) + rb1[m].astype(F32)

    sums(0, 4)

    total = gsum[pl.ds(pl.multiple_of(one * 16, 16), 16), :]
    for n, copy in enumerate(r_copies):
        copy.wait_recv()
        total += grow_in[n].astype(F32)
    gcol_in[two] = total.astype(BF16)

    def c_copy(d):
        where = along_two(d)
        return pltpu.make_async_remote_copy(src_ref=gcol_in.at[two], dst_ref=gcol_in.at[two],
                                            send_sem=c_send.at[d], recv_sem=c_recv.at[d], device_id=where, device_id_type=MESH)

    c_copies = [c_copy(d) for d in range(15)]
    each(c_copies, "start")
    sums(4, 8)
    each(c_copies, "wait_recv")
    total = gcol_in[0].astype(F32)
    for d in range(1, NC):
        total += gcol_in[d].astype(F32)
    gall[one] = (total * (1.0 / 256.0)).astype(BF16)

    def b_copy(d):
        to, where = along_one(d)
        return pltpu.make_async_remote_copy(src_ref=gall.at[one], dst_ref=gall.at[one],
                                            send_sem=b_send.at[d], recv_sem=b_recv.at[d], device_id=where, device_id_type=MESH)

    b_copies = [b_copy(d) for d in range(15)]
    each(b_copies, "start")

    each(y_copies, "wait_recv")
    back = acc[i]
    for m in range(7):
        back += yrecv[m].astype(F32)
    gf_ref[0] = jnp.dot(back.astype(BF16).T, wt[...], preferred_element_type=F32).astype(BF16)

    each(b_copies, "wait_recv")
    for d in range(NR):
        gw_ref[d * 16:(d + 1) * 16, :] = gall[d].astype(F32)

    each(sends + fsends + core_copies + y_copies + r_copies + c_copies + b_copies, "wait_send")


def shards(grad_out, pre_act, features, weight, tiles, live, block_row, block_col):
    vmem = pl.BlockSpec(memory_space=pltpu.VMEM)
    hbm = pl.BlockSpec(memory_space=pltpu.HBM)
    return pl.pallas_call(
        kernel,
        out_shape=(pltpu.VMEM((1, 256, F), BF16), pltpu.VMEM((F, F), F32)),
        in_specs=[hbm, hbm, hbm, hbm, hbm, pl.BlockSpec(memory_space=pltpu.SMEM), hbm, hbm],
        out_specs=(vmem, vmem),
        scratch_shapes=[
            pltpu.VMEM((256, F), BF16),
            pltpu.VMEM((256, F), BF16),
            pltpu.VMEM((F, F), BF16),
            pltpu.VMEM((1, 1, LISTED), jnp.int32),
            pltpu.VMEM((1, 1, LISTED), jnp.int32),
            pltpu.SemaphoreType.DMA((6,)),
            pltpu.VMEM((LISTED + 1, B, B), BF16),
            pltpu.VMEM((NB, F, B), BF16),
            pltpu.VMEM((NR, F, F), F32),
            pltpu.VMEM((8, B), jnp.int32),
            pltpu.SMEM((8, B), jnp.int32),
            pltpu.VMEM((NR, 256, F), BF16),
            pltpu.VMEM((F, F), BF16),
            pltpu.VMEM((NR, F, F), BF16),
            pltpu.VMEM((8, F, F), BF16),
            pltpu.VMEM((7, F, F), BF16),
            pltpu.VMEM((F, F), F32),
            pltpu.VMEM((F, F), BF16),
            pltpu.VMEM((NR, 16, F), BF16),
            pltpu.VMEM((NC, 16, F), BF16),
            pltpu.VMEM((NR, 16, F), BF16),
            pltpu.SemaphoreType.DMA,
            pltpu.SemaphoreType.DMA,
            pltpu.SemaphoreType.DMA((N_AG,)),
            pltpu.SemaphoreType.DMA((N_AG,)),
            pltpu.SemaphoreType.DMA((17,)),
            pltpu.SemaphoreType.DMA((17,)),
            pltpu.SemaphoreType.DMA((8,)),
            pltpu.SemaphoreType.DMA((8,)),
            pltpu.SemaphoreType.DMA((7,)),
            pltpu.SemaphoreType.DMA((7,)),
            pltpu.SemaphoreType.DMA((NR,)),
            pltpu.SemaphoreType.DMA((NR,)),
            pltpu.SemaphoreType.DMA((NC,)),
            pltpu.SemaphoreType.DMA((NC,)),
            pltpu.SemaphoreType.DMA((NR,)),
            pltpu.SemaphoreType.DMA((NR,)),
        ],
        compiler_params=pltpu.CompilerParams(collective_id=0, has_side_effects=True, vmem_limit_bytes=56 * 1024 * 1024),
        cost_estimate=pl.CostEstimate(flops=2 * 4096 * 4096 * 256, bytes_accessed=10 * 1024 * 1024, transcendentals=0),
    )(grad_out, pre_act, features, weight, tiles, live, block_row, block_col)


def solution(mesh):
    in_specs = (
        P(("row", "col"), None),
        P(("row", "col"), None),
        P("col", "row", None),
        P(),
        P("row", "col", None, None, None),
        P("row", "col"),
        P("row", "col", None),
        P("row", "col", None),
    )
    out_specs = (P("col", "row", None), P())
    return jax.shard_map(shards, mesh=mesh, in_specs=in_specs, out_specs=out_specs, check_vma=False)
```

```python
import functools

import jax
import jax.numpy as jnp
from jax import lax
from jax.experimental import pallas as pl
from jax.experimental.pallas import tpu as pltpu
from jax.sharding import PartitionSpec as P

MESH = pl.DeviceIdType.MESH
F32 = jnp.float32
BF16 = jnp.bfloat16

F = 256
B = 128
NB = 32
LISTED = 256
NR = 16
NC = 16
STEPS = 4

N_AG = 34


def kernel(go_hbm, pre_hbm, feat_hbm, w_hbm, tiles_ref, live_ref, brow_hbm, bcol_hbm,
           gf_ref, gw_ref,
           go_ref, pre_ref, w_ref, brow_ref, bcol_ref, in_sem,
           tiles_v, gt, acc, idx_v, idx_s, fv, wt,
           pb, rb1, yrecv,
           gsum, grow, grow_in, gcol_in, gall,
           tile_sem, idx_sem, ag_send, ag_recv, f_send, f_recv, s1_send, s1_recv, y_send, y_recv,
           r_send, r_recv, c_send, c_recv, b_send, b_recv):
    i = lax.axis_index("row")
    j = lax.axis_index("col")
    y, xh, c = i // 4, (i // 2) % 2, i % 2
    xl, z = j // 8, j % 8

    def row_of(yy, xx, cc):
        return (yy * 2 + xx) * 2 + cc

    z_up = (i, xl * 8 + (z + 1) % 8)
    z_dn = (i, xl * 8 + (z + 7) % 8)
    x_peer = (i, (1 - xl) * 8 + z)
    core_peer = (row_of(y, xh, 1 - c), j)
    y_up = (row_of((y + 1) % 4, xh, c), j)
    y_dn = (row_of((y + 3) % 4, xh, c), j)
    xh_peer = (row_of(y, 1 - xh, c), j)

    loads = [pltpu.make_async_copy(a, b, in_sem.at[k]) for k, (a, b) in enumerate((
        (go_hbm, go_ref), (pre_hbm, pre_ref), (brow_hbm, brow_ref), (bcol_hbm, bcol_ref), (feat_hbm.at[0], fv.at[i]), (w_hbm, w_ref)))]
    for load in loads:
        load.start()
    tile_copy = pltpu.make_async_copy(tiles_ref.at[0, 0], tiles_v.at[pl.ds(0, LISTED)], tile_sem)
    tile_copy.start()

    barrier = pltpu.get_barrier_semaphore()

    for near_by in (z_up, z_dn, x_peer, core_peer, y_up, y_dn, xh_peer):
        pl.semaphore_signal(barrier, inc=1, device_id=near_by, device_id_type=MESH)

    loads[0].wait()
    loads[1].wait()
    g = jnp.where(pre_ref[...] > 0, go_ref[...], jnp.zeros_like(go_ref[...]))
    gT = g.T
    gt[2 * j] = gT[:, :B]
    gt[2 * j + 1] = gT[:, B:]

    pl.semaphore_wait(barrier, 7)

    sends = []

    def blk(dz, cls):
        zz = (z + dz + 16) % 8
        side = xl if cls in "AB" else 1 - xl
        return 2 * (side * 8 + zz) + (1 if cls in "BQ" else 0)

    def send(block, half, target, k):
        if half is None:
            src = gt.at[block]
        else:
            src = gt.at[block, pl.ds(half * B, B)]
        d = pltpu.make_async_remote_copy(src_ref=src, dst_ref=src, send_sem=ag_send.at[k], recv_sem=ag_recv.at[k],
                                         device_id=target, device_id_type=MESH)
        d.start()
        sends.append(d)
        return d

    CLS = "BAP"
    handle = {}

    def push(cls, s, src_up, src_dn):
        ci = CLS.index(cls)
        half_u = 0 if s == STEPS else None
        half_d = 1 if s == STEPS else None
        handle[(cls, s, "u")] = send(blk(src_up, cls), half_u, z_up, ci * 4 + s - 1)
        handle[(cls, s, "d")] = send(blk(src_dn, cls), half_d, z_dn, 12 + ci * 4 + s - 1)

    xa = send(blk(0, "A"), None, x_peer, 24)
    push("B", 1, 0, 0)
    push("A", 1, 0, 0)
    xb = {0: [send(blk(0, "B"), None, x_peer, 25)]}

    for load in (loads[2], loads[3], loads[5]):
        load.wait()
    key = brow_ref[0] * NB + bcol_ref[0]
    lane = lax.broadcasted_iota(jnp.int32, (1, LISTED), 1)
    key = jnp.where(lane < live_ref[0, 0], key, -1)
    for h in range(2):
        kt = jnp.broadcast_to(key[:, h * B:(h + 1) * B], (B, B)).T
        number = lax.broadcasted_iota(jnp.int32, (B, B), 0) + h * B
        cell = lax.broadcasted_iota(jnp.int32, (B, B), 1)
        for q in range(8):
            found = jnp.where(kt == cell + q * B, number, LISTED)
            best = jnp.min(found, axis=0, keepdims=True)
            if h == 0:
                idx_v[q:q + 1, :] = best
            else:
                idx_v[q:q + 1, :] = jnp.minimum(idx_v[q:q + 1, :], best)
    idx_copy = pltpu.make_async_copy(idx_v, idx_s, idx_sem)
    idx_copy.start()
    tiles_v[LISTED] = jnp.zeros((B, B), BF16)
    wt[...] = w_ref[...].T

    def product(blocks, d):
        parts_l, parts_r = [], []
        for b in blocks:
            parts_l.append(gt[b])
            q, o = b // 4, (b % 4) * NB
            left = tiles_v[idx_s[q, o + 2 * d]]
            right = tiles_v[idx_s[q, o + 2 * d + 1]]
            parts_r.append(jnp.concatenate([left, right], axis=1))
        return jnp.dot(jnp.concatenate(parts_l, axis=1), jnp.concatenate(parts_r, axis=0), preferred_element_type=F32)

    def blocks_of(s):
        if s == 0 or s == STEPS:
            return [blk(s, k) for k in "ABPQ"]
        return [blk(t, k) for t in (s, -s) for k in "ABPQ"]

    def work(s, lo, hi, classes="ABPQ"):
        blocks = [blk(t, k) for t in ((s, -s) if s else (0,)) for k in classes]

        @pl.loop(lo, hi, unroll=hi - lo)
        def _(d):
            v = product(blocks, d)
            if s == 0:
                acc[d] = v
            else:
                acc[d] += v

    fsends = []

    def fcopy(row, half, target, k):
        src = fv.at[row] if half is None else fv.at[row, pl.ds(half * B, B)]
        d = pltpu.make_async_remote_copy(src_ref=src, dst_ref=src, send_sem=f_send.at[k], recv_sem=f_recv.at[k],
                                         device_id=target, device_id_type=MESH)
        d.start()
        fsends.append(d)
        return d

    def near(dy, q):
        return row_of((y + dy + 4) % 4, (xh + q) % 2, c)

    def fpush(q, k):
        return fcopy(near(0, q), None, y_up, k), fcopy(near(0, q), None, y_dn, k + 1)

    def fcore(dy, q, k):
        return fcopy(near(dy, q), None, core_peer, k)

    loads[4].wait()
    f_x = fcopy(i, None, xh_peer, 0)
    f_own = fpush(0, 1)
    to_core = [fcore(0, 0, 9)]
    f_far = {}
    f_xh = []

    def f_around(q):
        up, dn = (f_own, f_xh)[q]
        up.wait_recv()
        far_up = fcopy(near(-1, q), 0, y_up, 5 + 2 * q)
        dn.wait_recv()
        f_far[q] = (far_up, fcopy(near(1, q), 1, y_dn, 6 + 2 * q))
        to_core.append(fcore(-1, q, 11 + 2 * q))
        to_core.append(fcore(1, q, 12 + 2 * q))

    def f_end(q):
        for d in f_far[q]:
            d.wait_recv()
        to_core.append(fcore(2, q, 15 + q))

    def feature_step(s, cls):
        if (s, cls) == (1, "P"):
            f_around(0)
        elif (s, cls) == (2, "B"):
            f_x.wait_recv()
            f_xh.extend(fpush(1, 3))
            to_core.append(fcore(0, 1, 10))
        elif (s, cls) == (3, "A"):
            f_around(1)
            f_end(0)
        elif (s, cls) == (4, "P"):
            f_end(1)

    idx_copy.wait()
    tile_copy.wait()
    xa.wait_recv()
    push("P", 1, 0, 0)
    for s in range(1, STEPS + 1):
        for n, cls in enumerate(CLS):
            handle[(cls, s, "u")].wait_recv()
            handle[(cls, s, "d")].wait_recv()
            if s < STEPS:
                push(cls, s + 1, -s, s)
            if cls == "B":
                if s < STEPS:
                    xb[s] = [send(blk(-s, "B"), None, x_peer, 24 + 2 * s), send(blk(s, "B"), None, x_peer, 25 + 2 * s)]
                else:
                    xb[s] = [send(blk(s, "B"), 0, x_peer, 24 + 2 * s), send(blk(s, "B"), 1, x_peer, 25 + 2 * s)]
                for d in xb[s - 1]:
                    d.wait_recv()
            feature_step(s, cls)
            if n < 2:
                work(s - 1, 8 * n, 8 * n + 8, "PQ" if s > 1 else "ABPQ")
            elif s < STEPS:
                work(s, 0, NR, "AB")
    for d in xb[STEPS]:
        d.wait_recv()

    last = blocks_of(STEPS)
    ORDER = ((2, 1), (2, 0), (1, 1), (3, 1), (0, 1), (1, 0), (3, 0), (0, 0))

    def core_copy(m):
        return pltpu.make_async_remote_copy(src_ref=pb.at[dest(m, 1 - c)], dst_ref=rb1.at[m], send_sem=s1_send.at[m], recv_sem=s1_recv.at[m],
                                            device_id=core_peer, device_id_type=MESH)

    def dest(m, cc):
        dy, q = ORDER[m]
        return row_of((y + dy) % 4, (xh + q) % 2, cc)

    for m in range(8):
        d = dest(m, 1 - c)
        pb[d] = (acc[d] + product(last, d)).astype(BF16)
        core_copy(m).start()
    for m in range(8):
        d = dest(m, c)
        pb[d] = (acc[d] + product(last, d)).astype(BF16)

    def each(copies, what):
        for copy in copies:
            getattr(copy, what)()

    late = to_core.pop()
    spots = [near(dy, q) for dy, q in ((0, 0), (0, 1), (1, 0), (3, 0), (1, 1), (3, 1), (2, 0), (2, 1))]
    spots = [p + o for p in spots for o in (0, 1 - 2 * c)]
    for d in to_core:
        d.wait_recv()
    late.wait_recv()
    gt_sum = jnp.dot(jnp.concatenate([pb[p] for p in spots], axis=1), jnp.concatenate([fv[p] for p in spots], axis=0),
                     preferred_element_type=F32)
    gsum[...] = gt_sum.T
    grow[...] = gsum[...].astype(BF16)

    ONES = [(dy, p, k) for dy, p in ((2, 1), (1, 1), (3, 1), (2, 0), (0, 1), (1, 0), (3, 0), (0, 0)) for k in (1, 0)][:15]
    TWOS = [(4, 1), (3, 1), (5, 1), (4, 0), (2, 1), (6, 1), (1, 1), (7, 1), (3, 0), (5, 0), (0, 1), (2, 0), (6, 0), (1, 0), (7, 0)]
    one, two = (y * 2 + xl) * 2 + c, xh * 8 + z

    def along_one(d):
        dy, p, k = ONES[d]
        yy, pp, cc = (y + dy) % 4, (xl + p) % 2, (c + k) % 2
        return (yy * 2 + pp) * 2 + cc, (row_of(yy, xh, cc), pp * 8 + z)

    def along_two(d):
        dz, q = TWOS[d]
        return row_of(y, (xh + q) % 2, c), xl * 8 + (z + dz) % 8

    def r_copy(d):
        to, where = along_one(d)
        return pltpu.make_async_remote_copy(src_ref=grow.at[pl.ds(pl.multiple_of(to * 16, 16), 16)], dst_ref=grow_in.at[d],
                                            send_sem=r_send.at[d], recv_sem=r_recv.at[d], device_id=where, device_id_type=MESH)

    r_copies = [r_copy(d) for d in range(15)]
    each(r_copies, "start")

    def y_copy(m):
        dy, q = ORDER[m]
        return pltpu.make_async_remote_copy(src_ref=pb.at[dest(m, c)], dst_ref=yrecv.at[m], send_sem=y_send.at[m], recv_sem=y_recv.at[m],
                                            device_id=(dest(m, c), j), device_id_type=MESH)

    core_copies = [core_copy(m) for m in range(8)]
    y_copies = [y_copy(m) for m in range(7)]

    def sums(lo, hi):
        for m in range(lo, hi):
            core_copies[m].wait_recv()
            d = dest(m, c)
            if m < 7:
                pb[d] = (pb[d].astype(F32) + rb1[m].astype(F32)).astype(BF16)
                y_copies[m].start()
            else:
                acc[d] = pb[d].astype(F32) + rb1[m].astype(F32)

    sums(0, 4)

    total = gsum[pl.ds(pl.multiple_of(one * 16, 16), 16), :]
    for n, copy in enumerate(r_copies):
        copy.wait_recv()
        total += grow_in[n].astype(F32)
    gcol_in[two] = total.astype(BF16)

    def c_copy(d):
        where = along_two(d)
        return pltpu.make_async_remote_copy(src_ref=gcol_in.at[two], dst_ref=gcol_in.at[two],
                                            send_sem=c_send.at[d], recv_sem=c_recv.at[d], device_id=where, device_id_type=MESH)

    c_copies = [c_copy(d) for d in range(15)]
    each(c_copies, "start")
    sums(4, 8)
    each(c_copies, "wait_recv")
    total = gcol_in[0].astype(F32)
    for d in range(1, NC):
        total += gcol_in[d].astype(F32)
    gall[one] = (total * (1.0 / 256.0)).astype(BF16)

    def b_copy(d):
        to, where = along_one(d)
        return pltpu.make_async_remote_copy(src_ref=gall.at[one], dst_ref=gall.at[one],
                                            send_sem=b_send.at[d], recv_sem=b_recv.at[d], device_id=where, device_id_type=MESH)

    b_copies = [b_copy(d) for d in range(15)]
    each(b_copies, "start")

    each(y_copies, "wait_recv")
    back = acc[i]
    for m in range(7):
        back += yrecv[m].astype(F32)
    gf_ref[0] = jnp.dot(back.astype(BF16).T, wt[...], preferred_element_type=F32).astype(BF16)

    each(b_copies, "wait_recv")
    for d in range(NR):
        gw_ref[d * 16:(d + 1) * 16, :] = gall[d].astype(F32)

    each(sends + fsends + core_copies + y_copies + r_copies + c_copies + b_copies, "wait_send")


def shards(grad_out, pre_act, features, weight, tiles, live, block_row, block_col):
    vmem = pl.BlockSpec(memory_space=pltpu.VMEM)
    hbm = pl.BlockSpec(memory_space=pltpu.HBM)
    return pl.pallas_call(
        kernel,
        out_shape=(pltpu.VMEM((1, 256, F), BF16), pltpu.VMEM((F, F), F32)),
        in_specs=[hbm, hbm, hbm, hbm, hbm, pl.BlockSpec(memory_space=pltpu.SMEM), hbm, hbm],
        out_specs=(vmem, vmem),
        scratch_shapes=[
            pltpu.VMEM((256, F), BF16),
            pltpu.VMEM((256, F), BF16),
            pltpu.VMEM((F, F), BF16),
            pltpu.VMEM((1, 1, LISTED), jnp.int32),
            pltpu.VMEM((1, 1, LISTED), jnp.int32),
            pltpu.SemaphoreType.DMA((6,)),
            pltpu.VMEM((LISTED + 1, B, B), BF16),
            pltpu.VMEM((NB, F, B), BF16),
            pltpu.VMEM((NR, F, F), F32),
            pltpu.VMEM((8, B), jnp.int32),
            pltpu.SMEM((8, B), jnp.int32),
            pltpu.VMEM((NR, 256, F), BF16),
            pltpu.VMEM((F, F), BF16),
            pltpu.VMEM((NR, F, F), BF16),
            pltpu.VMEM((8, F, F), BF16),
            pltpu.VMEM((7, F, F), BF16),
            pltpu.VMEM((F, F), F32),
            pltpu.VMEM((F, F), BF16),
            pltpu.VMEM((NR, 16, F), BF16),
            pltpu.VMEM((NC, 16, F), BF16),
            pltpu.VMEM((NR, 16, F), BF16),
            pltpu.SemaphoreType.DMA,
            pltpu.SemaphoreType.DMA,
            pltpu.SemaphoreType.DMA((N_AG,)),
            pltpu.SemaphoreType.DMA((N_AG,)),
            pltpu.SemaphoreType.DMA((17,)),
            pltpu.SemaphoreType.DMA((17,)),
            pltpu.SemaphoreType.DMA((8,)),
            pltpu.SemaphoreType.DMA((8,)),
            pltpu.SemaphoreType.DMA((7,)),
            pltpu.SemaphoreType.DMA((7,)),
            pltpu.SemaphoreType.DMA((NR,)),
            pltpu.SemaphoreType.DMA((NR,)),
            pltpu.SemaphoreType.DMA((NC,)),
            pltpu.SemaphoreType.DMA((NC,)),
            pltpu.SemaphoreType.DMA((NR,)),
            pltpu.SemaphoreType.DMA((NR,)),
        ],
        compiler_params=pltpu.CompilerParams(collective_id=0, has_side_effects=True, vmem_limit_bytes=56 * 1024 * 1024),
        cost_estimate=pl.CostEstimate(flops=2 * 4096 * 4096 * 256, bytes_accessed=10 * 1024 * 1024, transcendentals=0),
    )(grad_out, pre_act, features, weight, tiles, live, block_row, block_col)


def solution(mesh):
    in_specs = (
        P(("row", "col"), None),
        P(("row", "col"), None),
        P("col", "row", None),
        P(),
        P("row", "col", None, None, None),
        P("row", "col"),
        P("row", "col", None),
        P("row", "col", None),
    )
    out_specs = (P("col", "row", None), P())
    return jax.shard_map(shards, mesh=mesh, in_specs=in_specs, out_specs=out_specs, check_vma=False)
```
